32 devices in a mesh: ctx: 8 (over z, y), chan: 4 (over x, core).
Axes of the slice: x: 2, y: 2, z: 4, core: 2. Of those that a mesh axis runs over, the one named last changes fastest.
Arguments:
- query_in: bfloat16 [1024, 8192], P(('ctx', 'chan')), may hold values from -6 to 6
- key_in: bfloat16 [1024, 8192], P(('ctx', 'chan')), may hold values from -6 to 6
- value_in: bfloat16 [1024, 8192], P(('ctx', 'chan')), may hold values from -6 to 6
- cotangent: bfloat16 [1024, 8192], P(('ctx', 'chan')), may hold values from -6 to 6
- residues: float32 [16, 8192], P(None, 'chan'), may hold values from -1.5 to 1.5
- decay_rate: float32 [16, 8192], P(None, 'chan'), may hold values from 1e-05 to 0.1
- short_weight: float32 [3, 3, 8192], P(None, None, 'chan'), may hold values from -3 to 3
- doc_lengths: int32 [8], replicated, may hold values from 1 to 512, 1024 in all
Outputs:
- output: bfloat16 [1024, 8192], P(('ctx', 'chan'))
- d_query_in: bfloat16 [1024, 8192], P(('ctx', 'chan'))
- d_key_in: bfloat16 [1024, 8192], P(('ctx', 'chan'))
- d_value_in: bfloat16 [1024, 8192], P(('ctx', 'chan'))
- d_resid: float32 [16, 8192], P(None, 'chan')
- d_short: float32 [3, 3, 8192], P(None, None, 'chan')
The draws below stay inside these ranges and needn't reach their ends.
Inputs may be any that keep to these rules, and one draw needn't show every extreme that they name: `doc_lengths`: the lengths of the 8 documents sum to 1024, and the longest has exactly 512 tokens.
All inputs are finite; a program needn't handle non-finite values.
Results may differ from the reference program's by a relative error of at most 0.001.
Values may be sent and summed in bfloat16 or wider, within the bound.
A program may use at most 128 MiB of HBM per device.

```python
import math
import jax
import jax.numpy as jnp
import numpy as np
from jax import lax

WIDTH = 8192
MODES = 16
SHORT = 3
DOCS = 8
TOKENS = 1024


def steps_of(own_key, shape, cuts, least, largest):
    def one(dim, blocks):
        steps = jax.random.uniform(jax.random.fold_in(jax.random.fold_in(own_key, 6), dim), (blocks,), jnp.float32, least / len(cuts), largest / len(cuts))
        return jnp.repeat(jnp.exp(steps), shape[dim] // blocks).reshape((-1,) + (1,) * (len(shape) - dim - 1))

    factor_of = one(*cuts[0])
    for cut in cuts[1:]:
        factor_of = factor_of * one(*cut)
    return factor_of


def profile(amount, total, most, slope):
    loads = [(1 << 20) // math.isqrt(grade ** slope) + 1 for grade in range(2, amount + 1)]
    spare, counts = total - most - (amount - 1), [1] * (amount - 1)
    while spare > 0:
        movable = [i for i in range(amount - 1) if counts[i] < most]
        pool, left = sum([loads[i] for i in movable]), spare
        for i in movable:
            extra = min(most - counts[i], max(1, left * loads[i] // pool), spare)
            counts[i] = counts[i] + extra
            spare = spare - extra
    return np.array([most] + counts)


def ragged_sizes(stream_key, number_of, total, most, slope):
    if number_of == 2:
        one = jax.random.randint(stream_key, (), max(1, total - most), min(most, total - 1) + 1)
        return jnp.stack([one, total - one])
    sizes = jnp.asarray(profile(number_of, total, most, slope), jnp.int32)
    twos = (number_of - 1) // 2
    giver, sink = sizes[1:1 + 2 * twos:2], sizes[2:2 + 2 * twos:2]
    margin = jnp.minimum(giver - 1, most - sink)
    passed = jax.random.randint(jax.random.fold_in(stream_key, 1), (twos,), 0, 1 << 20) % (margin + 1)
    sizes = sizes.at[1:1 + 2 * twos:2].set(giver - passed).at[2:2 + 2 * twos:2].set(sink + passed)
    return sizes[jax.random.permutation(jax.random.fold_in(stream_key, 2), number_of)]


def gaussian(key, extent, spread, most, shards=(), held_as=jnp.bfloat16):
    loudness = steps_of(key, extent, shards, -0.22, 0.18) if shards else 1.0
    result = jax.random.normal(key, extent, jnp.float32) * spread * loudness
    return jnp.minimum(jnp.maximum(result, -most), most).astype(held_as)


def setup_inputs(seed: int = 0) -> dict:
    arg_keys = jax.random.split(jax.random.key(seed), 9)
    query_in = gaussian(arg_keys[0], (TOKENS, WIDTH), 1.0, 6.0, ((0, 32),))
    key_in = gaussian(arg_keys[1], (TOKENS, WIDTH), 1.0, 6.0, ((0, 32),))
    value_in = gaussian(arg_keys[2], (TOKENS, WIDTH), 1.0, 6.0, ((0, 32),))
    cotangent = gaussian(arg_keys[3], (TOKENS, WIDTH), 1.0, 6.0, ((0, 32),))
    residues = gaussian(arg_keys[4], (MODES, WIDTH), 0.25, 1.5, ((1, 4),), jnp.float32)
    decay_rate = jnp.clip(jnp.exp(math.log(0.1) - 9.2103404 * jax.random.uniform(arg_keys[5], (MODES, WIDTH), jnp.float32) ** steps_of(arg_keys[5], (MODES, WIDTH), ((1, 4),), -0.2, 0.2)), 9.999999747378752e-06, 0.1)
    short_weight = gaussian(arg_keys[6], (3, SHORT, WIDTH), 0.6, 3.0, ((2, 4),), jnp.float32)
    doc_lengths = ragged_sizes(arg_keys[7], DOCS, TOKENS, TOKENS // 2, 2).astype(jnp.int32)
    return {"query_in": query_in, "key_in": key_in, "value_in": value_in, "cotangent": cotangent, "residues": residues, "decay_rate": decay_rate, "short_weight": short_weight, "doc_lengths": doc_lengths}


def doc_starts(doc_lengths):
    return (jnp.cumsum(doc_lengths) - doc_lengths).astype(jnp.int32)

def start_flags(positions, starts):
    hits = (positions[:, None] == starts[None, :]).astype(jnp.float32)
    return lax.optimization_barrier(jnp.sum(hits, axis=1))

def shift_down(values, count):
    padding = [(count, 0)] + [(0, 0)] * (values.ndim - 1)
    return jnp.pad(values, padding)[:values.shape[0]]

def featurize(row_block, taps, flagged):
    summed = taps[0][None, :] * row_block
    keep_mask = jnp.ones(row_block.shape[:1], jnp.float32)
    for offset in range(1, taps.shape[0]):
        keep_mask = keep_mask * (1.0 - shift_down(flagged, offset - 1))
        summed = summed + taps[offset][None, :] * (keep_mask[:, None] * shift_down(row_block, offset))
    return summed

def reference(query_in, key_in, value_in, cotangent, residues, decay_rate, short_weight, doc_lengths):
    starts = doc_starts(doc_lengths)
    positions = jnp.arange(TOKENS, dtype=jnp.int32)
    flagged = start_flags(positions, starts)

    def features(query_rows, key_rows, value_rows, taps):
        return (featurize(query_rows, taps[0], flagged), featurize(key_rows, taps[1], flagged), featurize(value_rows, taps[2], flagged))
    (query_feat, key_feat, value_feat), pullback = jax.vjp(features, query_in.astype(jnp.float32), key_in.astype(jnp.float32), value_in.astype(jnp.float32), short_weight)
    decays = jnp.exp(-decay_rate)
    kappa = jnp.sqrt(1.0 - jnp.exp(-2.0 * decay_rate))
    mixing = residues * kappa
    product = key_feat * value_feat
    grad_full = cotangent.astype(jnp.float32)
    grad_pre = grad_full * query_feat

    def forward_step(carry, inputs):
        states, accumulated = carry
        product_row, grad_row, flag_row = inputs
        states = decays * (1.0 - flag_row) * states + product_row[None, :]
        accumulated = accumulated + grad_row[None, :] * states
        return ((states, accumulated), lax.optimization_barrier(jnp.sum(mixing * states, axis=0)))
    zero_state = jnp.zeros(residues.shape, jnp.float32)
    (_, accumulated), filtered = lax.scan(forward_step, (zero_state, zero_state), (product, grad_pre, flagged))
    flags_next = jnp.concatenate([flagged[1:], jnp.ones((1,), jnp.float32)])

    def reverse_step(states, inputs):
        grad_row, flag_row = inputs
        states = decays * (1.0 - flag_row) * states + grad_row[None, :]
        return (states, lax.optimization_barrier(jnp.sum(mixing * states, axis=0)))
    _, grad_product = lax.scan(reverse_step, zero_state, (grad_pre, flags_next), reverse=True)
    output = (query_feat * filtered).astype(jnp.bfloat16)
    d_query, d_key, d_value, d_short = pullback((grad_full * filtered, grad_product * value_feat, grad_product * key_feat))
    d_resid = kappa * accumulated
    return (output, d_query.astype(jnp.bfloat16), d_key.astype(jnp.bfloat16), d_value.astype(jnp.bfloat16), d_resid, d_short)
```

```python
import functools

import jax
import jax.numpy as jnp
from jax import lax
from jax.experimental import pallas as pl
from jax.experimental.pallas import tpu as pltpu
from jax.sharding import PartitionSpec as P

MESH = pl.DeviceIdType.MESH
sub, lanes = 8, 128
wide = sub * lanes
step_rows = 4


def total_of(terms):
    terms = list(terms)
    while len(terms) > 1:
        paired = [a + b for a, b in zip(terms[::2], terms[1::2])]
        terms = paired + ([terms[-1]] if len(terms) % 2 else [])
    return terms[0]


def mixer(
    shape,
    flags, gates, reach, query_in, key_in, value_in, cotangent, table, mixing, kappa, taps,
    output, d_query, d_key, d_value, d_resid, d_short,
    inbox, stage, rows, grads, feats, product, grad_pre, d_feat, outbox,
    state_send, state_recv, part, shares, summed, whole,
    in_send, in_recv, local_sem, tail_send, tail_recv, far_send, far_recv,
    head_send, head_recv, out_send, out_recv, share_send, share_recv, whole_send, whole_recv,
):
    n, width, span, count, modes, tap_count, piece, chunks = shape
    own_rows = count // width
    pitch = stage.shape[1] // sub
    rim = tap_count - 1
    ctx = lax.axis_index("ctx")
    chan = lax.axis_index("chan")
    sources = (query_in, key_in, value_in, cotangent)
    targets = (output, d_query, d_key, d_value)

    def peer_chan(k):
        return lax.rem(chan + k, width)

    def at_chan(c):
        return (ctx, c)

    def at_ctx(c):
        return (c, chan)

    barrier = pltpu.get_barrier_semaphore()
    for k in range(1, width):
        pl.semaphore_signal(barrier, inc=1, device_id=at_chan(peer_chan(k)), device_id_type=MESH)

    def greet(k, carry):
        pl.semaphore_signal(barrier, inc=1, device_id=at_ctx(lax.rem(ctx + k, n)), device_id_type=MESH)
        return carry

    lax.fori_loop(1, n, greet, 0)
    pl.semaphore_wait(barrier, width - 1 + n - 1)

    def columns(owner, q):
        return pl.ds(pl.multiple_of((owner * chunks + q) * wide, wide), wide)

    def in_copy(q, a, k):
        peer = peer_chan(k)
        return pltpu.make_async_remote_copy(
            src_ref=sources[a].at[:, columns(peer, q)],
            dst_ref=inbox.at[a, q, chan],
            send_sem=in_send.at[q, a, k],
            recv_sem=in_recv.at[q, a, k],
            device_id=at_chan(peer),
            device_id_type=MESH,
        )

    def in_arrival(q, a, k):
        return pltpu.make_async_remote_copy(
            src_ref=sources[a].at[:, columns(chan, q)],
            dst_ref=inbox.at[a, q, lax.rem(chan + width - k, width)],
            send_sem=in_send.at[q, a, k],
            recv_sem=in_recv.at[q, a, k],
            device_id=at_chan(peer_chan(k)),
            device_id_type=MESH,
        )

    def in_local(q, a):
        return pltpu.make_async_copy(
            sources[a].at[:, columns(chan, q)], inbox.at[a, q, chan], local_sem.at[0, q, a]
        )

    for q in range(chunks):
        for a in range(4):
            for k in range(1, width):
                in_copy(q, a, k).start()
            in_local(q, a).start()

    def tail_copy(q, i):
        return pltpu.make_async_remote_copy(
            src_ref=rows.at[q, i, pl.ds(count, rim)],
            dst_ref=rows.at[q, i, pl.ds(0, rim)],
            send_sem=tail_send.at[q, i],
            recv_sem=tail_recv.at[q, i],
            device_id=at_ctx(lax.rem(ctx + 1, n)),
            device_id_type=MESH,
        )

    def head_copy(q, i):
        return pltpu.make_async_remote_copy(
            src_ref=d_feat.at[q, i, pl.ds(0, rim)],
            dst_ref=d_feat.at[q, i, pl.ds(count, rim)],
            send_sem=head_send.at[q, i],
            recv_sem=head_recv.at[q, i],
            device_id=at_ctx(lax.rem(ctx + n - 1, n)),
            device_id_type=MESH,
        )

    def far_copy(q, way, d):
        partner = lax.rem(ctx + d, n) if way == 0 else lax.rem(ctx + n - d, n)
        return pltpu.make_async_remote_copy(
            src_ref=state_send.at[q, way],
            dst_ref=state_recv.at[q, way, d - 1],
            send_sem=far_send.at[q, way, d - 1],
            recv_sem=far_recv.at[q, way, d - 1],
            device_id=at_ctx(partner),
            device_id_type=MESH,
        )

    def sends_far(way, d):
        return ctx + d < n if way == 0 else ctx >= d

    def gets_far(way, d):
        return ctx >= d if way == 0 else ctx + d < n

    def far_start(q, way):
        for d in range(1, span + 1):
            @pl.when(sends_far(way, d))
            def _():
                far_copy(q, way, d).start()

    def far_wait(q, way):
        for d in range(1, span + 1):
            @pl.when(gets_far(way, d))
            def _():
                far_copy(q, way, d).wait_recv()

            @pl.when(jnp.logical_not(gets_far(way, d)))
            def _():
                state_recv[q, way, d - 1] = jnp.zeros((modes, sub, lanes), jnp.float32)

    def mode_block(q):
        return pl.ds(q * sub, sub)

    def first_pass(q):
        for a in range(4):
            for k in range(1, width):
                in_arrival(q, a, k).wait_recv()
            in_local(q, a).wait()

        for a in range(4):
            def place(s, carry):
                for j in range(sub):
                    tile = inbox[a, q, s, :, pl.ds(j * lanes, lanes)].astype(jnp.float32)
                    stage[a, pl.ds(pl.multiple_of(j * pitch + s * own_rows, 8), own_rows), :] = tile
                return carry

            lax.fori_loop(0, width, place, 0)

        def lift(b, carry):
            for u in range(step_rows):
                t = b * step_rows + u
                for a in range(3):
                    rows[q, a, t + rim] = stage[a, pl.ds(t, sub, stride=pitch), :]
                grads[q, t] = stage[3, pl.ds(t, sub, stride=pitch), :]
            return carry

        lax.fori_loop(0, count // step_rows, lift, 0)
        for i in range(3):
            tail_copy(q, i).start()
        for i in range(3):
            tail_copy(q, i).wait_recv()

        decay = [table[0, m, mode_block(q), :] for m in range(modes)]
        tap = [[taps[i * tap_count + j, mode_block(q), :] for j in range(tap_count)] for i in range(3)]

        def featurize(b, states):
            for u in range(step_rows):
                t = b * step_rows + u
                made = []
                for i in range(3):
                    made.append(
                        tap[i][0] * rows[q, i, t + rim]
                        + total_of(
                            [
                                (gates[j, t] * tap[i][j]) * rows[q, i, t + rim - j]
                                for j in range(1, tap_count)
                            ]
                        )
                    )
                value = made[1] * made[2]
                for i in range(3):
                    feats[q, i, t] = made[i]
                product[q, t] = value
                grad_pre[q, t] = grads[q, t] * made[0]
                masked = gates[tap_count, t] * value
                states = tuple(decay[m] * states[m] + masked for m in range(modes))
            return states

        zeros = tuple(jnp.zeros((sub, lanes), jnp.float32) for _ in range(modes))
        ends = lax.fori_loop(0, count // step_rows, featurize, zeros)
        for m in range(modes):
            state_send[q, 0, m] = ends[m]
        far_start(q, 0)

        def back(b, states):
            for u in range(step_rows):
                t = count - 1 - b * step_rows - u
                masked = gates[0, t] * grad_pre[q, t]
                states = tuple(decay[m] * states[m] + masked for m in range(modes))
            return states

        ends = lax.fori_loop(0, count // step_rows, back, zeros)
        for m in range(modes):
            state_send[q, 1, m] = ends[m]
        far_start(q, 1)

    def entering(q, way):
        far_wait(q, way)
        carried = []
        for m in range(modes):
            power = table[0, m, mode_block(q), :]
            for _ in range(count.bit_length() - 1):
                power = power * power

            def nearer(s, value, m=m, power=power):
                d = span - s
                return power * value + reach[way, d - 1] * state_recv[q, way, d - 1, m]

            carried.append(lax.fori_loop(0, span, nearer, jnp.zeros((sub, lanes), jnp.float32)))
        return tuple(carried)

    def short_terms(q, i, t, grad):
        return [grad * rows[q, i, t + rim]] + [
            (gates[j, t] * grad) * rows[q, i, t + rim - j] for j in range(1, tap_count)
        ]

    def share_copy(q, k):
        peer = lax.rem(ctx + k, n)
        return pltpu.make_async_remote_copy(
            src_ref=part.at[q, peer],
            dst_ref=shares.at[q, k],
            send_sem=share_send.at[q, k],
            recv_sem=share_recv.at[q, k],
            device_id=at_ctx(peer),
            device_id_type=MESH,
        )

    def whole_copy(q, k):
        return pltpu.make_async_remote_copy(
            src_ref=summed.at[q],
            dst_ref=whole.at[q, ctx],
            send_sem=whole_send.at[q, k],
            recv_sem=whole_recv.at[q, k],
            device_id=at_ctx(lax.rem(ctx + k, n)),
            device_id_type=MESH,
        )

    def whole_arrival(q, k):
        return pltpu.make_async_remote_copy(
            src_ref=summed.at[q],
            dst_ref=whole.at[q, lax.rem(ctx + n - k, n)],
            send_sem=whole_send.at[q, k],
            recv_sem=whole_recv.at[q, k],
            device_id=at_ctx(lax.rem(ctx + k, n)),
            device_id_type=MESH,
        )

    def out_copy(q, a, k):
        peer = peer_chan(k)
        return pltpu.make_async_remote_copy(
            src_ref=outbox.at[a, q, peer],
            dst_ref=targets[a].at[:, columns(chan, q)],
            send_sem=out_send.at[q, a, k],
            recv_sem=out_recv.at[q, a, k],
            device_id=at_chan(peer),
            device_id_type=MESH,
        )

    def out_arrival(q, a, k):
        origin = lax.rem(chan + width - k, width)
        return pltpu.make_async_remote_copy(
            src_ref=outbox.at[a, q, origin],
            dst_ref=targets[a].at[:, columns(origin, q)],
            send_sem=out_send.at[q, a, k],
            recv_sem=out_recv.at[q, a, k],
            device_id=at_chan(peer_chan(k)),
            device_id_type=MESH,
        )

    def out_local(q, a):
        return pltpu.make_async_copy(
            outbox.at[a, q, chan], targets[a].at[:, columns(chan, q)], local_sem.at[1, q, a]
        )

    def send_out(q, a):
        def pack(s, carry):
            for j in range(sub):
                tile = stage[a, pl.ds(pl.multiple_of(j * pitch + s * own_rows, 8), own_rows), :]
                outbox[a, q, s, :, pl.ds(j * lanes, lanes)] = tile.astype(jnp.bfloat16)
            return carry

        lax.fori_loop(0, width, pack, 0)
        for k in range(1, width):
            out_copy(q, a, k).start()
        out_local(q, a).start()

    def put_part(q, index, value):
        part[q, index // piece, index % piece] = value

    def second_pass(q):
        mix = [mixing[m, mode_block(q), :] for m in range(modes)]
        tap = [[taps[i * tap_count + j, mode_block(q), :] for j in range(tap_count)] for i in range(3)]
        zero = jnp.zeros((sub, lanes), jnp.float32)
        carried = entering(q, 1)

        def reverse(b, carry):
            states, sums = carry
            for u in range(step_rows):
                t = count - 1 - b * step_rows - u
                flag = flags[t + 1]
                grad_row = grad_pre[q, t]
                states = tuple(
                    table[flag, m, mode_block(q), :] * states[m] + grad_row for m in range(modes)
                )
                mixed = total_of([mix[m] * states[m] for m in range(modes)])
                pair = (mixed * feats[q, 2, t], mixed * feats[q, 1, t])
                d_feat[q, 1, t] = pair[0]
                d_feat[q, 2, t] = pair[1]
                terms = short_terms(q, 1, t, pair[0]) + short_terms(q, 2, t, pair[1])
                sums = tuple(s + x for s, x in zip(sums, terms))
            return states, sums

        _, sums = lax.fori_loop(
            0, count // step_rows, reverse, (carried, (zero,) * (2 * tap_count))
        )
        head_copy(q, 1).start()
        head_copy(q, 2).start()
        for x in range(2 * tap_count):
            put_part(q, modes + tap_count + x, sums[x])
        carried = entering(q, 0)

        def advance(b, carry):
            states, found, sums = carry
            for u in range(step_rows):
                t = b * step_rows + u
                flag = flags[t]
                value = product[q, t]
                grad_row = grad_pre[q, t]
                states = tuple(
                    table[flag, m, mode_block(q), :] * states[m] + value for m in range(modes)
                )
                mixed = total_of([mix[m] * states[m] for m in range(modes)])
                found = tuple(found[m] + grad_row * states[m] for m in range(modes))
                stage[0, pl.ds(t, sub, stride=pitch), :] = feats[q, 0, t] * mixed
                grad = grads[q, t] * mixed
                d_feat[q, 0, t] = grad
                sums = tuple(s + x for s, x in zip(sums, short_terms(q, 0, t, grad)))
            return states, found, sums

        start = (carried, (zero,) * modes, (zero,) * tap_count)
        _, found, sums = lax.fori_loop(0, count // step_rows, advance, start)
        head_copy(q, 0).start()
        send_out(q, 0)
        for m in range(modes):
            put_part(q, m, kappa[m, mode_block(q), :] * found[m])
        for x in range(tap_count):
            put_part(q, modes + x, sums[x])
        for x in range(modes + 3 * tap_count, n * piece):
            put_part(q, x, zero)

        def spread(k, carry):
            share_copy(q, k).start()
            return carry

        lax.fori_loop(1, n, spread, 0)
        for i in (1, 2, 0):
            head_copy(q, i).wait_recv()

            def undo(b, carry):
                for u in range(step_rows):
                    t = b * step_rows + u
                    stage[1 + i, pl.ds(t, sub, stride=pitch), :] = tap[i][0] * d_feat[q, i, t] + total_of(
                        [
                            (gates[j, t + j] * tap[i][j]) * d_feat[q, i, t + j]
                            for j in range(1, tap_count)
                        ]
                    )
                return carry

            lax.fori_loop(0, count // step_rows, undo, 0)
            send_out(q, 1 + i)

    def gather(q):
        def take(k, carry):
            share_copy(q, k).wait_recv()
            return carry

        lax.fori_loop(1, n, take, 0)
        shares[q, 0] = part[q, ctx]

        def add(k, value):
            return value + shares[q, k]

        total = lax.fori_loop(1, n, add, shares[q, 0])
        summed[q] = total
        whole[q, ctx] = total

        def spread(k, carry):
            whole_copy(q, k).start()
            return carry

        lax.fori_loop(1, n, spread, 0)

    def write(q):
        def take(k, carry):
            whole_arrival(q, k).wait_recv()
            return carry

        lax.fori_loop(1, n, take, 0)
        for x in range(modes):
            value = whole[q, x // piece, x % piece]
            for j in range(sub):
                d_resid[pl.ds(x, 1), pl.ds((q * sub + j) * lanes, lanes)] = value[j : j + 1]
        for y in range(3 * tap_count):
            x = modes + y
            value = whole[q, x // piece, x % piece]
            for j in range(sub):
                d_short[pl.ds(y, 1), pl.ds((q * sub + j) * lanes, lanes)] = value[j : j + 1]

    for q in range(chunks):
        first_pass(q)
    for q in range(chunks):
        second_pass(q)
        if q:
            gather(q - 1)
    gather(chunks - 1)
    for q in range(chunks):
        write(q)

    for q in range(chunks):
        for a in range(4):
            for k in range(1, width):
                in_copy(q, a, k).wait_send()
                out_copy(q, a, k).wait_send()
                out_arrival(q, a, k).wait_recv()
            out_local(q, a).wait()
        for i in range(3):
            tail_copy(q, i).wait_send()
            head_copy(q, i).wait_send()
        for way in range(2):
            for d in range(1, span + 1):
                @pl.when(sends_far(way, d))
                def _():
                    far_copy(q, way, d).wait_send()

        def drain(k, carry):
            share_copy(q, k).wait_send()
            whole_copy(q, k).wait_send()
            return carry

        lax.fori_loop(1, n, drain, 0)


def shards(n, width, query_in, key_in, value_in, cotangent, residues, decay_rate, short_weight, doc_lengths):
    own_rows, channels = query_in.shape
    modes, local = residues.shape
    tap_count = short_weight.shape[1]
    rim = tap_count - 1
    count = own_rows * width
    chunks = local // wide
    tiles = local // lanes
    span = max(n // 2, 1)
    first_row = lax.axis_index("ctx") * count
    order = jnp.arange(doc_lengths.shape[0], dtype=jnp.int32)
    starts = jnp.sum(jnp.where(order[None, :] < order[:, None], doc_lengths[None, :], 0), axis=1)
    positions = first_row - rim + jnp.arange(count + 2 * rim, dtype=jnp.int32)
    hits = jnp.any(positions[:, None] == starts[None, :], axis=1)
    after = positions[rim:]
    gate_rows = []
    behind = (after < n * count) & (after >= 0)
    gate_rows_tail = []
    keep = behind
    for j in range(1, tap_count):
        keep = keep & ~hits[rim - j + 1 : rim - j + 1 + count + rim]
        gate_rows_tail.append(keep & (after >= j))
    inside = (starts[None, :] >= first_row) & (starts[None, :] <= after[:, None])
    gate_rows.append(~jnp.any(inside, axis=1))
    gate_rows += gate_rows_tail
    later = (starts[None, :] > after[:, None]) & (starts[None, :] < first_row + count)
    gate_rows.append(~jnp.any(later, axis=1))
    gates = jnp.stack(gate_rows).astype(jnp.float32)
    flags = hits[rim:].astype(jnp.int32)
    hop = jnp.arange(1, span + 1, dtype=jnp.int32)[:, None]
    early = (starts[None, :] >= first_row - (hop - 1) * count) & (starts[None, :] < first_row)
    late = (starts[None, :] >= first_row + count) & (starts[None, :] < first_row + hop * count)
    reach = jnp.stack([~jnp.any(early, axis=1), ~jnp.any(late, axis=1)]).astype(jnp.float32)

    decays = jnp.exp(-decay_rate)
    kappa = jnp.sqrt(1.0 - jnp.exp(-2.0 * decay_rate))
    mixing = residues * kappa
    table = jnp.stack([decays, jnp.zeros_like(decays)]).reshape(2, modes, tiles, lanes)
    mixing = mixing.reshape(modes, tiles, lanes)
    kappa = kappa.reshape(modes, tiles, lanes)
    taps = short_weight.reshape(3 * tap_count, tiles, lanes)

    pieces = modes + 3 * tap_count
    piece = -(-pieces // n)
    pitch = count + 8
    f32, bf16 = jnp.float32, jnp.bfloat16
    dma = pltpu.SemaphoreType.DMA
    anywhere = pl.BlockSpec(memory_space=pl.ANY)
    vmem = pl.BlockSpec(memory_space=pltpu.VMEM)
    smem = pl.BlockSpec(memory_space=pltpu.SMEM)
    shape = (n, width, span, count, modes, tap_count, piece, chunks)
    token = (sub, lanes)
    results = pl.pallas_call(
        functools.partial(mixer, shape),
        out_shape=[jax.ShapeDtypeStruct((own_rows, channels), bf16)] * 4
        + [
            jax.ShapeDtypeStruct((modes, local), f32),
            jax.ShapeDtypeStruct((3 * tap_count, local), f32),
        ],
        in_specs=[smem] * 3 + [anywhere] * 4 + [vmem] * 4,
        out_specs=[anywhere] * 4 + [vmem] * 2,
        scratch_shapes=[
            pltpu.VMEM((4, chunks, width, own_rows, wide), bf16),
            pltpu.VMEM((4, sub * pitch, lanes), f32),
            pltpu.VMEM((chunks, 3, count + rim) + token, f32),
            pltpu.VMEM((chunks, count) + token, f32),
            pltpu.VMEM((chunks, 3, count) + token, f32),
            pltpu.VMEM((chunks, count) + token, f32),
            pltpu.VMEM((chunks, count) + token, f32),
            pltpu.VMEM((chunks, 3, count + rim) + token, f32),
            pltpu.VMEM((4, chunks, width, own_rows, wide), bf16),
            pltpu.VMEM((chunks, 2, modes) + token, f32),
            pltpu.VMEM((chunks, 2, span, modes) + token, f32),
            pltpu.VMEM((chunks, n, piece) + token, f32),
            pltpu.VMEM((chunks, n, piece) + token, f32),
            pltpu.VMEM((chunks, piece) + token, f32),
            pltpu.VMEM((chunks, n, piece) + token, f32),
            dma((chunks, 4, width)),
            dma((chunks, 4, width)),
            dma((2, chunks, 4)),
            dma((chunks, 3)),
            dma((chunks, 3)),
            dma((chunks, 2, span)),
            dma((chunks, 2, span)),
            dma((chunks, 3)),
            dma((chunks, 3)),
            dma((chunks, 4, width)),
            dma((chunks, 4, width)),
            dma((chunks, n)),
            dma((chunks, n)),
            dma((chunks, n)),
            dma((chunks, n)),
        ],
        compiler_params=pltpu.CompilerParams(
            collective_id=0, has_side_effects=True, vmem_limit_bytes=48 * 1024 * 1024
        ),
    )(flags, gates, reach, query_in, key_in, value_in, cotangent, table, mixing, kappa, taps)
    return (*results[:5], results[5].reshape(short_weight.shape))


def solution(mesh):
    tokens = P(("ctx", "chan"), None)
    return jax.shard_map(
        functools.partial(shards, mesh.shape["ctx"], mesh.shape["chan"]),
        mesh=mesh,
        in_specs=(tokens,) * 4 + (P(None, "chan"), P(None, "chan"), P(None, None, "chan"), P()),
        out_specs=(tokens,) * 4 + (P(None, "chan"), P(None, None, "chan")),
        check_vma=False,
    )
```

```python
import functools

import jax
import jax.numpy as jnp
from jax import lax
from jax.experimental import pallas as pl
from jax.experimental.pallas import tpu as pltpu
from jax.sharding import PartitionSpec as P

MESH = pl.DeviceIdType.MESH
sub, lanes = 8, 128
wide = sub * lanes
step_rows = 8
most_vmem = 60 * 1024 * 1024


def total_of(terms):
    terms = list(terms)
    while len(terms) > 1:
        paired = [a + b for a, b in zip(terms[::2], terms[1::2])]
        terms = paired + ([terms[-1]] if len(terms) % 2 else [])
    return terms[0]


def mixer(
    shape,
    lengths, query_in, key_in, value_in, cotangent, decays, mixing_in, kappa_in, weights,
    output, d_query, d_key, d_value, d_resid, d_short,
    inbox, stage, rows, grads, feats, product, grad_pre, d_feat, outbox,
    state_send, state_recv, part, shares, summed, whole,
    flags, gates, reach, flat, table, mixing, kappa, taps,
    in_send, in_recv, local_sem, tail_send, tail_recv, far_send, far_recv,
    head_send, head_recv, out_send, out_recv, share_send, share_recv, whole_send, whole_recv,
):
    n, width, span, count, modes, tap_count, piece, chunks = shape
    own_rows = count // width
    pitch = stage.shape[1] // sub
    rim = tap_count - 1
    ctx = lax.axis_index("ctx")
    chan = lax.axis_index("chan")
    sources = (query_in, key_in, value_in, cotangent)
    targets = (output, d_query, d_key, d_value)

    def peer_chan(k):
        return lax.rem(chan + k, width)

    def at_chan(c):
        return (ctx, c)

    def at_ctx(c):
        return (c, chan)

    barrier = pltpu.get_barrier_semaphore()
    for k in range(1, width):
        pl.semaphore_signal(barrier, inc=1, device_id=at_chan(peer_chan(k)), device_id_type=MESH)

    def greet(k, carry):
        pl.semaphore_signal(barrier, inc=1, device_id=at_ctx(lax.rem(ctx + k, n)), device_id_type=MESH)
        return carry

    lax.fori_loop(1, n, greet, 0)
    pl.semaphore_wait(barrier, width - 1 + n - 1)

    def columns(owner, q):
        return pl.ds(pl.multiple_of((owner * chunks + q) * wide, wide), wide)

    def in_copy(q, a, k):
        peer = peer_chan(k)
        return pltpu.make_async_remote_copy(
            src_ref=sources[a].at[:, columns(peer, q)],
            dst_ref=inbox.at[a, q, chan],
            send_sem=in_send.at[q, a, k],
            recv_sem=in_recv.at[q, a, k],
            device_id=at_chan(peer),
            device_id_type=MESH,
        )

    def in_arrival(q, a, k):
        return pltpu.make_async_remote_copy(
            src_ref=sources[a].at[:, columns(chan, q)],
            dst_ref=inbox.at[a, q, lax.rem(chan + width - k, width)],
            send_sem=in_send.at[q, a, k],
            recv_sem=in_recv.at[q, a, k],
            device_id=at_chan(peer_chan(k)),
            device_id_type=MESH,
        )

    def in_local(q, a):
        return pltpu.make_async_copy(
            sources[a].at[:, columns(chan, q)], inbox.at[a, q, chan], local_sem.at[0, q, a]
        )

    def in_start(q):
        for a in range(4):
            for k in range(1, width):
                in_copy(q, a, k).start()
            in_local(q, a).start()

    in_start(0)

    first = ctx * count
    starts = [jnp.int32(0)]
    for d in range(lengths.shape[0] - 1):
        starts.append(starts[-1] + lengths[d])

    def mark(x, carry):
        position = first - rim + x
        flags[x] = jnp.minimum(sum(jnp.where(position == s, 1, 0) for s in starts), 1)
        return carry

    lax.fori_loop(0, count + 2 * rim, mark, 0)

    def open_gates(t, seen):
        seen = seen + flags[t + rim]
        gates[0, t] = jnp.where(seen == 0, 1.0, 0.0)
        crossed = jnp.where(first + t < n * count, 0, 1)
        for j in range(1, tap_count):
            crossed = crossed + flags[t + rim - j + 1]
            gates[j, t] = jnp.where(crossed == 0, 1.0, 0.0)
        return seen

    lax.fori_loop(0, count + rim, open_gates, jnp.int32(0))

    def open_ends(x, seen):
        t = count - 1 - x
        gates[tap_count, t] = jnp.where(seen == 0, 1.0, 0.0)
        return seen + flags[t + rim]

    lax.fori_loop(0, count, open_ends, jnp.int32(0))

    def open_reach(d, carry):
        low = first - d * count
        high = first + (d + 1) * count
        early = sum(jnp.where((s >= low) & (s < first), 1, 0) for s in starts)
        late = sum(jnp.where((s >= first + count) & (s < high), 1, 0) for s in starts)
        reach[0, d] = jnp.where(early == 0, 1.0, 0.0)
        reach[1, d] = jnp.where(late == 0, 1.0, 0.0)
        return carry

    lax.fori_loop(0, span, open_reach, 0)

    tiles = chunks * sub
    for x, origin in enumerate((decays, mixing_in, kappa_in)):
        for j in range(tiles):
            flat[x, pl.ds(j * modes, modes), :] = origin[:, pl.ds(j * lanes, lanes)]
    for m in range(modes):
        for q in range(chunks):
            where = pl.ds(q * sub, sub)
            picked = pl.ds(q * sub * modes + m, sub, stride=modes)
            table[0, m, where, :] = flat[0, picked, :]
            table[1, m, where, :] = jnp.zeros((sub, lanes), jnp.float32)
            mixing[m, where, :] = flat[1, picked, :]
            kappa[m, where, :] = flat[2, picked, :]
    for i in range(3):
        for j in range(tap_count):
            for x in range(tiles):
                taps[i * tap_count + j, pl.ds(x, 1), :] = weights[i, pl.ds(j, 1), pl.ds(x * lanes, lanes)]

    def tail_copy(q, i):
        return pltpu.make_async_remote_copy(
            src_ref=rows.at[q, i, pl.ds(count, rim)],
            dst_ref=rows.at[q, i, pl.ds(0, rim)],
            send_sem=tail_send.at[q, i],
            recv_sem=tail_recv.at[q, i],
            device_id=at_ctx(lax.rem(ctx + 1, n)),
            device_id_type=MESH,
        )

    def head_copy(q, i):
        return pltpu.make_async_remote_copy(
            src_ref=d_feat.at[q, i, pl.ds(0, rim)],
            dst_ref=d_feat.at[q, i, pl.ds(count, rim)],
            send_sem=head_send.at[q, i],
            recv_sem=head_recv.at[q, i],
            device_id=at_ctx(lax.rem(ctx + n - 1, n)),
            device_id_type=MESH,
        )

    def far_copy(q, way, d):
        partner = lax.rem(ctx + d, n) if way == 0 else lax.rem(ctx + n - d, n)
        return pltpu.make_async_remote_copy(
            src_ref=state_send.at[q, way],
            dst_ref=state_recv.at[q, way, d - 1],
            send_sem=far_send.at[q, way, d - 1],
            recv_sem=far_recv.at[q, way, d - 1],
            device_id=at_ctx(partner),
            device_id_type=MESH,
        )

    def sends_far(way, d):
        return ctx + d < n if way == 0 else ctx >= d

    def gets_far(way, d):
        return ctx >= d if way == 0 else ctx + d < n

    def far_start(q, way):
        for d in range(1, span + 1):
            @pl.when(sends_far(way, d))
            def _():
                far_copy(q, way, d).start()

    def far_wait(q, way):
        for d in range(1, span + 1):
            @pl.when(gets_far(way, d))
            def _():
                far_copy(q, way, d).wait_recv()

            @pl.when(jnp.logical_not(gets_far(way, d)))
            def _():
                state_recv[q, way, d - 1] = jnp.zeros((modes, sub, lanes), jnp.float32)

    def mode_block(q):
        return pl.ds(q * sub, sub)

    def first_pass(q):
        for a in range(4):
            for k in range(1, width):
                in_arrival(q, a, k).wait_recv()
            in_local(q, a).wait()
            if a == 3 and q + 1 < chunks:
                in_start(q + 1)

        for a in range(4):
            def place(s, carry):
                for j in range(sub):
                    tile = inbox[a, q, s, :, pl.ds(j * lanes, lanes)].astype(jnp.float32)
                    stage[a, pl.ds(pl.multiple_of(j * pitch + s * own_rows, 8), own_rows), :] = tile
                return carry

            lax.fori_loop(0, width, place, 0)

        def lift(b, carry):
            for u in range(step_rows):
                t = b * step_rows + u
                for a in range(3):
                    rows[q, a, t + rim] = stage[a, pl.ds(t, sub, stride=pitch), :]
                grads[q, t] = stage[3, pl.ds(t, sub, stride=pitch), :]
            return carry

        lax.fori_loop(0, count // step_rows, lift, 0)
        for i in range(3):
            tail_copy(q, i).start()
        decay = [table[0, m, mode_block(q), :] for m in range(modes)]
        tap = [[taps[i * tap_count + j, mode_block(q), :] for j in range(tap_count)] for i in range(3)]

        def feature(i, t):
            return tap[i][0] * rows[q, i, t + rim] + total_of(
                [
                    (gates[j, t] * tap[i][j]) * rows[q, i, t + rim - j]
                    for j in range(1, tap_count)
                ]
            )

        def featurize(b, states):
            for u in range(step_rows):
                t = b * step_rows + u
                made = (feature(1, t), feature(2, t))
                value = made[0] * made[1]
                feats[q, 1, t] = made[0]
                feats[q, 2, t] = made[1]
                product[q, t] = value
                masked = gates[tap_count, t] * value
                states = tuple(decay[m] * states[m] + masked for m in range(modes))
            return states

        zeros = tuple(jnp.zeros((sub, lanes), jnp.float32) for _ in range(modes))
        def back(b, states):
            for u in range(step_rows):
                t = count - 1 - b * step_rows - u
                query = feature(0, t)
                feats[q, 0, t] = query
                value = grads[q, t] * query
                grad_pre[q, t] = value
                masked = gates[0, t] * value
                states = tuple(decay[m] * states[m] + masked for m in range(modes))
            return states

        last = count // step_rows - 1
        ends = lax.fori_loop(0, last, back, zeros)
        for i in range(3):
            tail_copy(q, i).wait_recv()
        ends = lax.fori_loop(last, last + 1, back, ends)
        for m in range(modes):
            state_send[q, 1, m] = ends[m]
        far_start(q, 1)
        ends = lax.fori_loop(0, count // step_rows, featurize, zeros)
        for m in range(modes):
            state_send[q, 0, m] = ends[m]
        far_start(q, 0)

    def entering(q, way):
        far_wait(q, way)
        carried = []
        for m in range(modes):
            power = table[0, m, mode_block(q), :]
            for _ in range(count.bit_length() - 1):
                power = power * power

            def nearer(s, value, m=m, power=power):
                d = span - s
                return power * value + reach[way, d - 1] * state_recv[q, way, d - 1, m]

            carried.append(lax.fori_loop(0, span, nearer, jnp.zeros((sub, lanes), jnp.float32)))
        return tuple(carried)

    def short_terms(q, i, t, grad):
        return [grad * rows[q, i, t + rim]] + [
            (gates[j, t] * grad) * rows[q, i, t + rim - j] for j in range(1, tap_count)
        ]

    def share_copy(q, k):
        peer = lax.rem(ctx + k, n)
        return pltpu.make_async_remote_copy(
            src_ref=part.at[q, peer],
            dst_ref=shares.at[q, k],
            send_sem=share_send.at[q, k],
            recv_sem=share_recv.at[q, k],
            device_id=at_ctx(peer),
            device_id_type=MESH,
        )

    def whole_copy(q, k):
        return pltpu.make_async_remote_copy(
            src_ref=summed.at[q],
            dst_ref=whole.at[q, ctx],
            send_sem=whole_send.at[q, k],
            recv_sem=whole_recv.at[q, k],
            device_id=at_ctx(lax.rem(ctx + k, n)),
            device_id_type=MESH,
        )

    def whole_arrival(q, k):
        return pltpu.make_async_remote_copy(
            src_ref=summed.at[q],
            dst_ref=whole.at[q, lax.rem(ctx + n - k, n)],
            send_sem=whole_send.at[q, k],
            recv_sem=whole_recv.at[q, k],
            device_id=at_ctx(lax.rem(ctx + k, n)),
            device_id_type=MESH,
        )

    def out_copy(q, a, k):
        peer = peer_chan(k)
        return pltpu.make_async_remote_copy(
            src_ref=outbox.at[a, q, peer],
            dst_ref=targets[a].at[:, columns(chan, q)],
            send_sem=out_send.at[q, a, k],
            recv_sem=out_recv.at[q, a, k],
            device_id=at_chan(peer),
            device_id_type=MESH,
        )

    def out_arrival(q, a, k):
        origin = lax.rem(chan + width - k, width)
        return pltpu.make_async_remote_copy(
            src_ref=outbox.at[a, q, origin],
            dst_ref=targets[a].at[:, columns(origin, q)],
            send_sem=out_send.at[q, a, k],
            recv_sem=out_recv.at[q, a, k],
            device_id=at_chan(peer_chan(k)),
            device_id_type=MESH,
        )

    def out_local(q, a):
        return pltpu.make_async_copy(
            outbox.at[a, q, chan], targets[a].at[:, columns(chan, q)], local_sem.at[1, q, a]
        )

    def send_out(q, a):
        def pack(s, carry):
            for j in range(sub):
                tile = stage[a, pl.ds(pl.multiple_of(j * pitch + s * own_rows, 8), own_rows), :]
                outbox[a, q, s, :, pl.ds(j * lanes, lanes)] = tile.astype(jnp.bfloat16)
            return carry

        lax.fori_loop(0, width, pack, 0)
        for k in range(1, width):
            out_copy(q, a, k).start()
        out_local(q, a).start()

    def put_part(q, index, value):
        part[q, index // piece, index % piece] = value

    def second_pass(q):
        mix = [mixing[m, mode_block(q), :] for m in range(modes)]
        tap = [[taps[i * tap_count + j, mode_block(q), :] for j in range(tap_count)] for i in range(3)]
        zero = jnp.zeros((sub, lanes), jnp.float32)
        carried = entering(q, 1)

        def reverse(b, carry):
            states, sums = carry
            for u in range(step_rows):
                t = count - 1 - b * step_rows - u
                flag = flags[t + rim + 1]
                grad_row = grad_pre[q, t]
                states = tuple(
                    table[flag, m, mode_block(q), :] * states[m] + grad_row for m in range(modes)
                )
                mixed = total_of([mix[m] * states[m] for m in range(modes)])
                pair = (mixed * feats[q, 2, t], mixed * feats[q, 1, t])
                d_feat[q, 1, t] = pair[0]
                d_feat[q, 2, t] = pair[1]
                terms = short_terms(q, 1, t, pair[0]) + short_terms(q, 2, t, pair[1])
                sums = tuple(s + x for s, x in zip(sums, terms))
            return states, sums

        _, sums = lax.fori_loop(
            0, count // step_rows, reverse, (carried, (zero,) * (2 * tap_count))
        )
        head_copy(q, 1).start()
        head_copy(q, 2).start()
        for x in range(2 * tap_count):
            put_part(q, modes + tap_count + x, sums[x])
        carried = entering(q, 0)

        def advance(b, carry):
            states, found, sums = carry
            for u in range(step_rows):
                t = b * step_rows + u
                flag = flags[t + rim]
                value = product[q, t]
                grad_row = grad_pre[q, t]
                states = tuple(
                    table[flag, m, mode_block(q), :] * states[m] + value for m in range(modes)
                )
                mixed = total_of([mix[m] * states[m] for m in range(modes)])
                found = tuple(found[m] + grad_row * states[m] for m in range(modes))
                stage[0, pl.ds(t, sub, stride=pitch), :] = feats[q, 0, t] * mixed
                grad = grads[q, t] * mixed
                d_feat[q, 0, t] = grad
                sums = tuple(s + x for s, x in zip(sums, short_terms(q, 0, t, grad)))
            return states, found, sums

        start = (carried, (zero,) * modes, (zero,) * tap_count)
        start = lax.fori_loop(0, 1, advance, start)
        head_copy(q, 0).start()
        _, found, sums = lax.fori_loop(1, count // step_rows, advance, start)
        send_out(q, 0)
        for m in range(modes):
            put_part(q, m, kappa[m, mode_block(q), :] * found[m])
        for x in range(tap_count):
            put_part(q, modes + x, sums[x])
        for x in range(modes + 3 * tap_count, n * piece):
            put_part(q, x, zero)

        def spread(k, carry):
            share_copy(q, k).start()
            return carry

        lax.fori_loop(1, n, spread, 0)
        for i in (1, 2, 0):
            head_copy(q, i).wait_recv()

            def undo(b, carry):
                for u in range(step_rows):
                    t = b * step_rows + u
                    stage[1 + i, pl.ds(t, sub, stride=pitch), :] = tap[i][0] * d_feat[q, i, t] + total_of(
                        [
                            (gates[j, t + j] * tap[i][j]) * d_feat[q, i, t + j]
                            for j in range(1, tap_count)
                        ]
                    )
                return carry

            lax.fori_loop(0, count // step_rows, undo, 0)
            send_out(q, 1 + i)

    def gather(q):
        def take(k, carry):
            share_copy(q, k).wait_recv()
            return carry

        lax.fori_loop(1, n, take, 0)
        shares[q, 0] = part[q, ctx]

        def add(k, value):
            return value + shares[q, k]

        total = lax.fori_loop(1, n, add, shares[q, 0])
        summed[q] = total
        whole[q, ctx] = total

        def spread(k, carry):
            whole_copy(q, k).start()
            return carry

        lax.fori_loop(1, n, spread, 0)

    def write(q):
        def take(k, carry):
            whole_arrival(q, k).wait_recv()
            return carry

        lax.fori_loop(1, n, take, 0)
        for x in range(modes):
            value = whole[q, x // piece, x % piece]
            for j in range(sub):
                d_resid[pl.ds(x, 1), pl.ds((q * sub + j) * lanes, lanes)] = value[j : j + 1]
        for y in range(3 * tap_count):
            x = modes + y
            value = whole[q, x // piece, x % piece]
            for j in range(sub):
                d_short[y // tap_count, pl.ds(y % tap_count, 1), pl.ds((q * sub + j) * lanes, lanes)] = value[j : j + 1]

    for q in range(chunks):
        first_pass(q)
    for q in range(chunks):
        second_pass(q)
        if q:
            gather(q - 1)
    gather(chunks - 1)
    for q in range(chunks):
        write(q)

    for q in range(chunks):
        for a in range(4):
            for k in range(1, width):
                in_copy(q, a, k).wait_send()
                out_copy(q, a, k).wait_send()
                out_arrival(q, a, k).wait_recv()
            out_local(q, a).wait()
        for i in range(3):
            tail_copy(q, i).wait_send()
            head_copy(q, i).wait_send()
        for way in range(2):
            for d in range(1, span + 1):
                @pl.when(sends_far(way, d))
                def _():
                    far_copy(q, way, d).wait_send()

        def drain(k, carry):
            share_copy(q, k).wait_send()
            whole_copy(q, k).wait_send()
            return carry

        lax.fori_loop(1, n, drain, 0)


def hand_over(*refs):
    copies = [pltpu.make_async_copy(refs[x], refs[6 + x], refs[12].at[x]) for x in range(6)]
    for copy in copies:
        copy.start()
    for copy in copies:
        copy.wait()


def shards(n, width, query_in, key_in, value_in, cotangent, residues, decay_rate, short_weight, doc_lengths):
    own_rows, channels = query_in.shape
    modes, local = residues.shape
    tap_count = short_weight.shape[1]
    rim = tap_count - 1
    count = own_rows * width
    chunks = local // wide
    tiles = local // lanes
    span = max(n // 2, 1)
    decays = jnp.exp(-decay_rate)
    kappa = jnp.sqrt(1.0 - jnp.exp(-2.0 * decay_rate))
    mixing = residues * kappa
    pieces = modes + 3 * tap_count
    piece = -(-pieces // n)
    pitch = count + 8
    f32, bf16 = jnp.float32, jnp.bfloat16
    dma = pltpu.SemaphoreType.DMA
    anywhere = pl.BlockSpec(memory_space=pltpu.HBM)
    vmem = pl.BlockSpec(memory_space=pltpu.VMEM)
    smem = pl.BlockSpec(memory_space=pltpu.SMEM)
    shape = (n, width, span, count, modes, tap_count, piece, chunks)
    token = (sub, lanes)
    results = pl.pallas_call(
        functools.partial(mixer, shape),
        out_shape=[jax.ShapeDtypeStruct((own_rows, channels), bf16)] * 4
        + [
            jax.ShapeDtypeStruct((modes, local), f32),
            jax.ShapeDtypeStruct(short_weight.shape, f32),
        ],
        in_specs=[smem] + [anywhere] * 4 + [vmem] * 4,
        out_specs=[anywhere] * 4 + [vmem] * 2,
        scratch_shapes=[
            pltpu.VMEM((4, chunks, width, own_rows, wide), bf16),
            pltpu.VMEM((4, sub * pitch, lanes), f32),
            pltpu.VMEM((chunks, 3, count + rim) + token, f32),
            pltpu.VMEM((chunks, count) + token, f32),
            pltpu.VMEM((chunks, 3, count) + token, f32),
            pltpu.VMEM((chunks, count) + token, f32),
            pltpu.VMEM((chunks, count) + token, f32),
            pltpu.VMEM((chunks, 3, count + rim) + token, f32),
            pltpu.VMEM((4, chunks, width, own_rows, wide), bf16),
            pltpu.VMEM((chunks, 2, modes) + token, f32),
            pltpu.VMEM((chunks, 2, span, modes) + token, f32),
            pltpu.VMEM((chunks, n, piece) + token, f32),
            pltpu.VMEM((chunks, n, piece) + token, f32),
            pltpu.VMEM((chunks, piece) + token, f32),
            pltpu.VMEM((chunks, n, piece) + token, f32),
            pltpu.SMEM((count + 2 * rim,), jnp.int32),
            pltpu.SMEM((tap_count + 1, count + rim), f32),
            pltpu.SMEM((2, span), f32),
            pltpu.VMEM((3, tiles * modes, lanes), f32),
            pltpu.VMEM((2, modes, tiles, lanes), f32),
            pltpu.VMEM((modes, tiles, lanes), f32),
            pltpu.VMEM((modes, tiles, lanes), f32),
            pltpu.VMEM((3 * tap_count, tiles, lanes), f32),
            dma((chunks, 4, width)),
            dma((chunks, 4, width)),
            dma((2, chunks, 4)),
            dma((chunks, 3)),
            dma((chunks, 3)),
            dma((chunks, 2, span)),
            dma((chunks, 2, span)),
            dma((chunks, 3)),
            dma((chunks, 3)),
            dma((chunks, 4, width)),
            dma((chunks, 4, width)),
            dma((chunks, n)),
            dma((chunks, n)),
            dma((chunks, n)),
            dma((chunks, n)),
        ],
        compiler_params=pltpu.CompilerParams(
            collective_id=0, has_side_effects=True, vmem_limit_bytes=most_vmem
        ),
    )(doc_lengths, query_in, key_in, value_in, cotangent, decays, mixing, kappa, short_weight)
    return pl.pallas_call(
        hand_over,
        out_shape=[jax.ShapeDtypeStruct(r.shape, r.dtype) for r in results],
        in_specs=[vmem] * 6,
        out_specs=[anywhere] * 6,
        scratch_shapes=[dma((6,))],
        compiler_params=pltpu.CompilerParams(vmem_limit_bytes=most_vmem),
    )(*results)


def solution(mesh):
    tokens = P(("ctx", "chan"), None)
    return jax.shard_map(
        functools.partial(shards, mesh.shape["ctx"], mesh.shape["chan"]),
        mesh=mesh,
        in_specs=(tokens,) * 4 + (P(None, "chan"), P(None, "chan"), P(None, None, "chan"), P()),
        out_specs=(tokens,) * 4 + (P(None, "chan"), P(None, None, "chan")),
        check_vma=False,
    )
```

```python
import functools

import jax
import jax.numpy as jnp
from jax import lax
from jax.experimental import pallas as pl
from jax.experimental.pallas import tpu as pltpu
from jax.sharding import PartitionSpec as P

MESH = pl.DeviceIdType.MESH
sub, lanes = 8, 128
wide = sub * lanes
step_rows = 8
most_vmem = 60 * 1024 * 1024


def total_of(terms):
    terms = list(terms)
    while len(terms) > 1:
        paired = [a + b for a, b in zip(terms[::2], terms[1::2])]
        terms = paired + ([terms[-1]] if len(terms) % 2 else [])
    return terms[0]


def mixer(
    shape,
    lengths, query_in, key_in, value_in, cotangent, decays, mixing_in, kappa_in, weights,
    output, d_query, d_key, d_value, d_resid, d_short,
    inbox, stage, rows, grads, feats, product, grad_pre, d_feat, outbox,
    state_send, state_recv, part, shares, summed, whole,
    flags, gates, reach, flat, table, mixing, kappa, taps,
    in_send, in_recv, local_sem, tail_send, tail_recv, far_send, far_recv,
    head_send, head_recv, out_send, out_recv, share_send, share_recv, whole_send, whole_recv,
):
    n, width, span, count, modes, tap_count, piece, chunks = shape
    own_rows = count // width
    pitch = stage.shape[1] // sub
    rim = tap_count - 1
    ctx = lax.axis_index("ctx")
    chan = lax.axis_index("chan")
    sources = (query_in, key_in, value_in, cotangent)
    targets = (output, d_query, d_key, d_value)

    def peer_chan(k):
        return lax.rem(chan + k, width)

    def at_chan(c):
        return (ctx, c)

    def at_ctx(c):
        return (c, chan)

    barrier = pltpu.get_barrier_semaphore()
    for k in range(1, width):
        pl.semaphore_signal(barrier, inc=1, device_id=at_chan(peer_chan(k)), device_id_type=MESH)

    def greet(k, carry):
        pl.semaphore_signal(barrier, inc=1, device_id=at_ctx(lax.rem(ctx + k, n)), device_id_type=MESH)
        return carry

    lax.fori_loop(1, n, greet, 0)
    pl.semaphore_wait(barrier, width - 1 + n - 1)

    def columns(owner, q):
        return pl.ds(pl.multiple_of((owner * chunks + q) * wide, wide), wide)

    def in_copy(q, a, k):
        peer = peer_chan(k)
        return pltpu.make_async_remote_copy(
            src_ref=sources[a].at[:, columns(peer, q)],
            dst_ref=inbox.at[a, q, chan],
            send_sem=in_send.at[q, a, k],
            recv_sem=in_recv.at[q, a, k],
            device_id=at_chan(peer),
            device_id_type=MESH,
        )

    def in_arrival(q, a, k):
        return pltpu.make_async_remote_copy(
            src_ref=sources[a].at[:, columns(chan, q)],
            dst_ref=inbox.at[a, q, lax.rem(chan + width - k, width)],
            send_sem=in_send.at[q, a, k],
            recv_sem=in_recv.at[q, a, k],
            device_id=at_chan(peer_chan(k)),
            device_id_type=MESH,
        )

    def in_local(q, a):
        return pltpu.make_async_copy(
            sources[a].at[:, columns(chan, q)], inbox.at[a, q, chan], local_sem.at[0, q, a]
        )

    def in_start(q):
        for a in range(4):
            for k in sorted(range(1, width), key=lambda k: abs(2 * k - width)):
                in_copy(q, a, k).start()
            in_local(q, a).start()

    in_start(0)

    first = ctx * count
    starts = [jnp.int32(0)]
    for d in range(lengths.shape[0] - 1):
        starts.append(starts[-1] + lengths[d])

    def mark(x, carry):
        position = first - rim + x
        flags[x] = jnp.minimum(sum(jnp.where(position == s, 1, 0) for s in starts), 1)
        return carry

    lax.fori_loop(0, count + 2 * rim, mark, 0)

    def open_gates(t, seen):
        seen = seen + flags[t + rim]
        gates[0, t] = jnp.where(seen == 0, 1.0, 0.0)
        crossed = jnp.where(first + t < n * count, 0, 1)
        for j in range(1, tap_count):
            crossed = crossed + flags[t + rim - j + 1]
            gates[j, t] = jnp.where(crossed == 0, 1.0, 0.0)
        return seen

    lax.fori_loop(0, count + rim, open_gates, jnp.int32(0))

    def open_ends(x, seen):
        t = count - 1 - x
        gates[tap_count, t] = jnp.where(seen == 0, 1.0, 0.0)
        return seen + flags[t + rim]

    lax.fori_loop(0, count, open_ends, jnp.int32(0))

    def open_reach(d, carry):
        low = first - d * count
        high = first + (d + 1) * count
        early = sum(jnp.where((s >= low) & (s < first), 1, 0) for s in starts)
        late = sum(jnp.where((s >= first + count) & (s < high), 1, 0) for s in starts)
        reach[0, d] = jnp.where(early == 0, 1.0, 0.0)
        reach[1, d] = jnp.where(late == 0, 1.0, 0.0)
        return carry

    lax.fori_loop(0, span, open_reach, 0)

    tiles = chunks * sub
    for x, origin in enumerate((decays, mixing_in, kappa_in)):
        for j in range(tiles):
            flat[x, pl.ds(j * modes, modes), :] = origin[:, pl.ds(j * lanes, lanes)]
    for m in range(modes):
        for q in range(chunks):
            where = pl.ds(q * sub, sub)
            picked = pl.ds(q * sub * modes + m, sub, stride=modes)
            table[0, m, where, :] = flat[0, picked, :]
            table[1, m, where, :] = jnp.zeros((sub, lanes), jnp.float32)
            mixing[m, where, :] = flat[1, picked, :]
            kappa[m, where, :] = flat[2, picked, :]
    for i in range(3):
        for j in range(tap_count):
            for x in range(tiles):
                taps[i * tap_count + j, pl.ds(x, 1), :] = weights[i, pl.ds(j, 1), pl.ds(x * lanes, lanes)]

    def tail_copy(q, i):
        return pltpu.make_async_remote_copy(
            src_ref=rows.at[q, i, pl.ds(count, rim)],
            dst_ref=rows.at[q, i, pl.ds(0, rim)],
            send_sem=tail_send.at[q, i],
            recv_sem=tail_recv.at[q, i],
            device_id=at_ctx(lax.rem(ctx + 1, n)),
            device_id_type=MESH,
        )

    def head_copy(q, i):
        return pltpu.make_async_remote_copy(
            src_ref=d_feat.at[q, i, pl.ds(0, rim)],
            dst_ref=d_feat.at[q, i, pl.ds(count, rim)],
            send_sem=head_send.at[q, i],
            recv_sem=head_recv.at[q, i],
            device_id=at_ctx(lax.rem(ctx + n - 1, n)),
            device_id_type=MESH,
        )

    def far_copy(q, way, d):
        partner = lax.rem(ctx + d, n) if way == 0 else lax.rem(ctx + n - d, n)
        return pltpu.make_async_remote_copy(
            src_ref=state_send.at[q, way],
            dst_ref=state_recv.at[q, way, d - 1],
            send_sem=far_send.at[q, way, d - 1],
            recv_sem=far_recv.at[q, way, d - 1],
            device_id=at_ctx(partner),
            device_id_type=MESH,
        )

    def sends_far(way, d):
        return ctx + d < n if way == 0 else ctx >= d

    def gets_far(way, d):
        return ctx >= d if way == 0 else ctx + d < n

    def far_start(q, way):
        for d in range(1, span + 1):
            @pl.when(sends_far(way, d))
            def _():
                far_copy(q, way, d).start()

    def far_wait(q, way):
        for d in range(1, span + 1):
            @pl.when(gets_far(way, d))
            def _():
                far_copy(q, way, d).wait_recv()

            @pl.when(jnp.logical_not(gets_far(way, d)))
            def _():
                state_recv[q, way, d - 1] = jnp.zeros((modes, sub, lanes), jnp.float32)

    def mode_block(q):
        return pl.ds(q * sub, sub)

    def first_pass(q):
        for a in range(4):
            for k in range(1, width):
                in_arrival(q, a, k).wait_recv()
            in_local(q, a).wait()
            if a == 3 and q + 1 < chunks:
                in_start(q + 1)

        for a in range(4):
            def place(s, carry):
                for j in range(sub):
                    tile = inbox[a, q, s, :, pl.ds(j * lanes, lanes)].astype(jnp.float32)
                    stage[a, pl.ds(pl.multiple_of(j * pitch + s * own_rows, 8), own_rows), :] = tile
                return carry

            lax.fori_loop(0, width, place, 0)

        def lift(b, carry):
            for u in range(step_rows):
                t = b * step_rows + u
                for a in range(3):
                    rows[q, a, t + rim] = stage[a, pl.ds(t, sub, stride=pitch), :]
                grads[q, t] = stage[3, pl.ds(t, sub, stride=pitch), :]
            return carry

        lax.fori_loop(0, count // step_rows, lift, 0)
        for i in range(3):
            tail_copy(q, i).start()
        decay = [table[0, m, mode_block(q), :] for m in range(modes)]
        tap = [[taps[i * tap_count + j, mode_block(q), :] for j in range(tap_count)] for i in range(3)]

        def feature(i, t):
            return tap[i][0] * rows[q, i, t + rim] + total_of(
                [
                    (gates[j, t] * tap[i][j]) * rows[q, i, t + rim - j]
                    for j in range(1, tap_count)
                ]
            )

        def featurize(b, states):
            for u in range(step_rows):
                t = b * step_rows + u
                made = (feature(1, t), feature(2, t))
                value = made[0] * made[1]
                feats[q, 1, t] = made[0]
                feats[q, 2, t] = made[1]
                product[q, t] = value
                masked = gates[tap_count, t] * value
                states = tuple(decay[m] * states[m] + masked for m in range(modes))
            return states

        zeros = tuple(jnp.zeros((sub, lanes), jnp.float32) for _ in range(modes))
        def back(b, states):
            for u in range(step_rows):
                t = count - 1 - b * step_rows - u
                query = feature(0, t)
                feats[q, 0, t] = query
                value = grads[q, t] * query
                grad_pre[q, t] = value
                masked = gates[0, t] * value
                states = tuple(decay[m] * states[m] + masked for m in range(modes))
            return states

        last = count // step_rows - 1
        ends = lax.fori_loop(0, last, back, zeros)
        for i in range(3):
            tail_copy(q, i).wait_recv()
        ends = lax.fori_loop(last, last + 1, back, ends)
        for m in range(modes):
            state_send[q, 1, m] = ends[m]
        far_start(q, 1)
        ends = lax.fori_loop(0, count // step_rows, featurize, zeros)
        for m in range(modes):
            state_send[q, 0, m] = ends[m]
        far_start(q, 0)

    def entering(q, way):
        far_wait(q, way)
        carried = []
        for m in range(modes):
            power = table[0, m, mode_block(q), :]
            for _ in range(count.bit_length() - 1):
                power = power * power

            def nearer(s, value, m=m, power=power):
                d = span - s
                return power * value + reach[way, d - 1] * state_recv[q, way, d - 1, m]

            carried.append(lax.fori_loop(0, span, nearer, jnp.zeros((sub, lanes), jnp.float32)))
        return tuple(carried)

    def short_terms(q, i, t, grad):
        return [grad * rows[q, i, t + rim]] + [
            (gates[j, t] * grad) * rows[q, i, t + rim - j] for j in range(1, tap_count)
        ]

    def share_copy(q, k):
        peer = lax.rem(ctx + k, n)
        return pltpu.make_async_remote_copy(
            src_ref=part.at[q, peer],
            dst_ref=shares.at[q, k],
            send_sem=share_send.at[q, k],
            recv_sem=share_recv.at[q, k],
            device_id=at_ctx(peer),
            device_id_type=MESH,
        )

    def whole_copy(q, k):
        return pltpu.make_async_remote_copy(
            src_ref=summed.at[q],
            dst_ref=whole.at[q, ctx],
            send_sem=whole_send.at[q, k],
            recv_sem=whole_recv.at[q, k],
            device_id=at_ctx(lax.rem(ctx + k, n)),
            device_id_type=MESH,
        )

    def whole_arrival(q, k):
        return pltpu.make_async_remote_copy(
            src_ref=summed.at[q],
            dst_ref=whole.at[q, lax.rem(ctx + n - k, n)],
            send_sem=whole_send.at[q, k],
            recv_sem=whole_recv.at[q, k],
            device_id=at_ctx(lax.rem(ctx + k, n)),
            device_id_type=MESH,
        )

    def out_copy(q, a, k):
        peer = peer_chan(k)
        return pltpu.make_async_remote_copy(
            src_ref=outbox.at[a, q, peer],
            dst_ref=targets[a].at[:, columns(chan, q)],
            send_sem=out_send.at[q, a, k],
            recv_sem=out_recv.at[q, a, k],
            device_id=at_chan(peer),
            device_id_type=MESH,
        )

    def out_arrival(q, a, k):
        origin = lax.rem(chan + width - k, width)
        return pltpu.make_async_remote_copy(
            src_ref=outbox.at[a, q, origin],
            dst_ref=targets[a].at[:, columns(origin, q)],
            send_sem=out_send.at[q, a, k],
            recv_sem=out_recv.at[q, a, k],
            device_id=at_chan(peer_chan(k)),
            device_id_type=MESH,
        )

    def out_local(q, a):
        return pltpu.make_async_copy(
            outbox.at[a, q, chan], targets[a].at[:, columns(chan, q)], local_sem.at[1, q, a]
        )

    def send_out(q, a):
        def pack(s, carry):
            for j in range(sub):
                tile = stage[a, pl.ds(pl.multiple_of(j * pitch + s * own_rows, 8), own_rows), :]
                outbox[a, q, s, :, pl.ds(j * lanes, lanes)] = tile.astype(jnp.bfloat16)
            return carry

        lax.fori_loop(0, width, pack, 0)
        for k in sorted(range(1, width), key=lambda k: abs(2 * k - width)):
            out_copy(q, a, k).start()
        out_local(q, a).start()

    def put_part(q, index, value):
        part[q, index // piece, index % piece] = value

    def second_pass(q):
        mix = [mixing[m, mode_block(q), :] for m in range(modes)]
        tap = [[taps[i * tap_count + j, mode_block(q), :] for j in range(tap_count)] for i in range(3)]
        zero = jnp.zeros((sub, lanes), jnp.float32)
        carried = entering(q, 1)

        def reverse(b, carry):
            states, sums = carry
            for u in range(step_rows):
                t = count - 1 - b * step_rows - u
                flag = flags[t + rim + 1]
                grad_row = grad_pre[q, t]
                states = tuple(
                    table[flag, m, mode_block(q), :] * states[m] + grad_row for m in range(modes)
                )
                mixed = total_of([mix[m] * states[m] for m in range(modes)])
                pair = (mixed * feats[q, 2, t], mixed * feats[q, 1, t])
                d_feat[q, 1, t] = pair[0]
                d_feat[q, 2, t] = pair[1]
                terms = short_terms(q, 1, t, pair[0]) + short_terms(q, 2, t, pair[1])
                sums = tuple(s + x for s, x in zip(sums, terms))
            return states, sums

        _, sums = lax.fori_loop(
            0, count // step_rows, reverse, (carried, (zero,) * (2 * tap_count))
        )
        head_copy(q, 1).start()
        head_copy(q, 2).start()
        for x in range(2 * tap_count):
            put_part(q, modes + tap_count + x, sums[x])
        carried = entering(q, 0)

        def advance(b, carry):
            states, found, sums = carry
            for u in range(step_rows):
                t = b * step_rows + u
                flag = flags[t + rim]
                value = product[q, t]
                grad_row = grad_pre[q, t]
                states = tuple(
                    table[flag, m, mode_block(q), :] * states[m] + value for m in range(modes)
                )
                mixed = total_of([mix[m] * states[m] for m in range(modes)])
                found = tuple(found[m] + grad_row * states[m] for m in range(modes))
                stage[0, pl.ds(t, sub, stride=pitch), :] = feats[q, 0, t] * mixed
                grad = grads[q, t] * mixed
                d_feat[q, 0, t] = grad
                sums = tuple(s + x for s, x in zip(sums, short_terms(q, 0, t, grad)))
            return states, found, sums

        start = (carried, (zero,) * modes, (zero,) * tap_count)
        start = lax.fori_loop(0, 1, advance, start)
        head_copy(q, 0).start()
        _, found, sums = lax.fori_loop(1, count // step_rows, advance, start)
        send_out(q, 0)
        for m in range(modes):
            put_part(q, m, kappa[m, mode_block(q), :] * found[m])
        for x in range(tap_count):
            put_part(q, modes + x, sums[x])
        for x in range(modes + 3 * tap_count, n * piece):
            put_part(q, x, zero)

        def spread(k, carry):
            share_copy(q, k).start()
            return carry

        lax.fori_loop(1, n, spread, 0)
        for i in (1, 2, 0):
            head_copy(q, i).wait_recv()

            def undo(b, carry):
                for u in range(step_rows):
                    t = b * step_rows + u
                    stage[1 + i, pl.ds(t, sub, stride=pitch), :] = tap[i][0] * d_feat[q, i, t] + total_of(
                        [
                            (gates[j, t + j] * tap[i][j]) * d_feat[q, i, t + j]
                            for j in range(1, tap_count)
                        ]
                    )
                return carry

            lax.fori_loop(0, count // step_rows, undo, 0)
            send_out(q, 1 + i)

    def gather(q):
        def take(k, carry):
            share_copy(q, k).wait_recv()
            return carry

        lax.fori_loop(1, n, take, 0)
        shares[q, 0] = part[q, ctx]

        def add(k, value):
            return value + shares[q, k]

        total = lax.fori_loop(1, n, add, shares[q, 0])
        summed[q] = total
        whole[q, ctx] = total

        def spread(k, carry):
            whole_copy(q, k).start()
            return carry

        lax.fori_loop(1, n, spread, 0)

    def write(q):
        def take(k, carry):
            whole_arrival(q, k).wait_recv()
            return carry

        lax.fori_loop(1, n, take, 0)
        for x in range(modes):
            value = whole[q, x // piece, x % piece]
            for j in range(sub):
                d_resid[pl.ds(x, 1), pl.ds((q * sub + j) * lanes, lanes)] = value[j : j + 1]
        for y in range(3 * tap_count):
            x = modes + y
            value = whole[q, x // piece, x % piece]
            for j in range(sub):
                d_short[y // tap_count, pl.ds(y % tap_count, 1), pl.ds((q * sub + j) * lanes, lanes)] = value[j : j + 1]

    for q in range(chunks):
        first_pass(q)
    for q in range(chunks):
        second_pass(q)
        if q:
            gather(q - 1)
    gather(chunks - 1)
    for q in range(chunks):
        write(q)

    for q in range(chunks):
        for a in range(4):
            for k in range(1, width):
                in_copy(q, a, k).wait_send()
                out_copy(q, a, k).wait_send()
                out_arrival(q, a, k).wait_recv()
            out_local(q, a).wait()
        for i in range(3):
            tail_copy(q, i).wait_send()
            head_copy(q, i).wait_send()
        for way in range(2):
            for d in range(1, span + 1):
                @pl.when(sends_far(way, d))
                def _():
                    far_copy(q, way, d).wait_send()

        def drain(k, carry):
            share_copy(q, k).wait_send()
            whole_copy(q, k).wait_send()
            return carry

        lax.fori_loop(1, n, drain, 0)


def hand_over(*refs):
    copies = [pltpu.make_async_copy(refs[x], refs[6 + x], refs[12].at[x]) for x in range(6)]
    for copy in copies:
        copy.start()
    for copy in copies:
        copy.wait()


def shards(n, width, query_in, key_in, value_in, cotangent, residues, decay_rate, short_weight, doc_lengths):
    own_rows, channels = query_in.shape
    modes, local = residues.shape
    tap_count = short_weight.shape[1]
    rim = tap_count - 1
    count = own_rows * width
    chunks = local // wide
    tiles = local // lanes
    span = max(n // 2, 1)
    decays = jnp.exp(-decay_rate)
    kappa = jnp.sqrt(1.0 - jnp.exp(-2.0 * decay_rate))
    mixing = residues * kappa
    pieces = modes + 3 * tap_count
    piece = -(-pieces // n)
    pitch = count + 8
    f32, bf16 = jnp.float32, jnp.bfloat16
    dma = pltpu.SemaphoreType.DMA
    anywhere = pl.BlockSpec(memory_space=pltpu.HBM)
    vmem = pl.BlockSpec(memory_space=pltpu.VMEM)
    smem = pl.BlockSpec(memory_space=pltpu.SMEM)
    shape = (n, width, span, count, modes, tap_count, piece, chunks)
    token = (sub, lanes)
    results = pl.pallas_call(
        functools.partial(mixer, shape),
        out_shape=[jax.ShapeDtypeStruct((own_rows, channels), bf16)] * 4
        + [
            jax.ShapeDtypeStruct((modes, local), f32),
            jax.ShapeDtypeStruct(short_weight.shape, f32),
        ],
        in_specs=[smem] + [anywhere] * 4 + [vmem] * 4,
        out_specs=[anywhere] * 4 + [vmem] * 2,
        scratch_shapes=[
            pltpu.VMEM((4, chunks, width, own_rows, wide), bf16),
            pltpu.VMEM((4, sub * pitch, lanes), f32),
            pltpu.VMEM((chunks, 3, count + rim) + token, f32),
            pltpu.VMEM((chunks, count) + token, f32),
            pltpu.VMEM((chunks, 3, count) + token, f32),
            pltpu.VMEM((chunks, count) + token, f32),
            pltpu.VMEM((chunks, count) + token, f32),
            pltpu.VMEM((chunks, 3, count + rim) + token, f32),
            pltpu.VMEM((4, chunks, width, own_rows, wide), bf16),
            pltpu.VMEM((chunks, 2, modes) + token, f32),
            pltpu.VMEM((chunks, 2, span, modes) + token, f32),
            pltpu.VMEM((chunks, n, piece) + token, f32),
            pltpu.VMEM((chunks, n, piece) + token, f32),
            pltpu.VMEM((chunks, piece) + token, f32),
            pltpu.VMEM((chunks, n, piece) + token, f32),
            pltpu.SMEM((count + 2 * rim,), jnp.int32),
            pltpu.SMEM((tap_count + 1, count + rim), f32),
            pltpu.SMEM((2, span), f32),
            pltpu.VMEM((3, tiles * modes, lanes), f32),
            pltpu.VMEM((2, modes, tiles, lanes), f32),
            pltpu.VMEM((modes, tiles, lanes), f32),
            pltpu.VMEM((modes, tiles, lanes), f32),
            pltpu.VMEM((3 * tap_count, tiles, lanes), f32),
            dma((chunks, 4, width)),
            dma((chunks, 4, width)),
            dma((2, chunks, 4)),
            dma((chunks, 3)),
            dma((chunks, 3)),
            dma((chunks, 2, span)),
            dma((chunks, 2, span)),
            dma((chunks, 3)),
            dma((chunks, 3)),
            dma((chunks, 4, width)),
            dma((chunks, 4, width)),
            dma((chunks, n)),
            dma((chunks, n)),
            dma((chunks, n)),
            dma((chunks, n)),
        ],
        compiler_params=pltpu.CompilerParams(
            collective_id=0, has_side_effects=True, vmem_limit_bytes=most_vmem
        ),
    )(doc_lengths, query_in, key_in, value_in, cotangent, decays, mixing, kappa, short_weight)
    return pl.pallas_call(
        hand_over,
        out_shape=[jax.ShapeDtypeStruct(r.shape, r.dtype) for r in results],
        in_specs=[vmem] * 6,
        out_specs=[anywhere] * 6,
        scratch_shapes=[dma((6,))],
        compiler_params=pltpu.CompilerParams(vmem_limit_bytes=most_vmem),
    )(*results)


def solution(mesh):
    tokens = P(("ctx", "chan"), None)
    return jax.shard_map(
        functools.partial(shards, mesh.shape["ctx"], mesh.shape["chan"]),
        mesh=mesh,
        in_specs=(tokens,) * 4 + (P(None, "chan"), P(None, "chan"), P(None, None, "chan"), P()),
        out_specs=(tokens,) * 4 + (P(None, "chan"), P(None, None, "chan")),
        check_vma=False,
    )
```
